256 devices in a mesh: dp: 4 (over x_lo, core), uly: 4 (over y), blk: 16 (over z, x_hi).
Axes of the slice: x: 4 (x_hi: 2, x_lo: 2; x = x_hi * 2 + x_lo), y: 4, z: 8, core: 2. Of those that a mesh axis runs over, the one named last changes fastest.
Arguments:
- q_tok: bfloat16 [4, 8192, 1536], P('dp', ('blk', 'uly')), may hold values from -5 to 5
- k_tok: bfloat16 [4, 8192, 1536], P('dp', ('blk', 'uly')), may hold values from -5 to 5
- v_tok: bfloat16 [4, 8192, 1536], P('dp', ('blk', 'uly')), may hold values from -6 to 6
- d_y: bfloat16 [4, 8192, 3072], P('dp', ('blk', 'uly')), may hold values from -8 to 8
- gate: float32 [4, 3072], P('dp'), may hold values from 0.3 to 3
- w_out: bfloat16 [3072, 1536], P('blk', 'uly'), may hold values from -0.15625 to 0.15625
Outputs:
- grad_q: bfloat16 [4, 8192, 1536], P('dp', ('blk', 'uly'))
- grad_k: bfloat16 [4, 8192, 1536], P('dp', ('blk', 'uly'))
- grad_v: bfloat16 [4, 8192, 1536], P('dp', ('blk', 'uly'))
- grad_w: float32 [3072, 1536], P('blk', 'uly')
The draws below stay inside these ranges and needn't reach their ends.
All inputs are finite; a program needn't handle non-finite values.
Results may differ from the reference program's by a relative error of at most 0.022.
Values may be sent and summed in bfloat16 or wider, within the bound.
No kernel may reach another device: no remote copies, remote signals or barrier semaphores. Data moves between devices by JAX's collectives and lax.ppermute only.
A program may use at most 64 MiB of HBM per device.

```python
import math
import jax
import jax.numpy as jnp
from jax import lax

D = 3072
HDIM = 128
HEADS = 12
SEQS = 4
BLOCK = 512
SEQ = 8192
HDH = 1536
N_BLK = 16


def draw_q_tok(key, part):
    key = jax.random.fold_in(key, 3)
    return jnp.clip(jax.random.normal(key, (SEQS, SEQ, HDH), jnp.float32), -5.0, 5.0).astype(jnp.bfloat16)


def draw_k_tok(key, part):
    key = jax.random.fold_in(key, 5)
    return jnp.clip(jax.random.normal(key, (SEQS, SEQ, HDH), jnp.float32), -5.0, 5.0).astype(jnp.bfloat16)


def strengthened(values, own_key, source, target, blocks, factor):
    def block_of(dim):
        return (jnp.arange(values.shape[dim]) // (values.shape[dim] // blocks)).reshape((-1,) + (1,) * (values.ndim - 1 - dim))

    first = jax.random.permutation(own_key, blocks)[block_of(target)]
    other_side = (block_of(target) + blocks // 2) % blocks
    return jnp.where((block_of(source) == first) | (block_of(source) == other_side), factor * values, values)


def level_of(key, shape, cuts, low, top_value):
    level, own = 1.0, jax.random.fold_in(key, 6)
    for axis_at, shards_of in cuts:
        steps = jnp.exp(jax.random.uniform(jax.random.fold_in(own, axis_at), (shards_of,), jnp.float32, low / len(cuts), top_value / len(cuts)))
        level = level * jnp.repeat(steps, shape[axis_at] // shards_of).reshape([-1 if axis == axis_at else 1 for axis in range(len(shape))])
    return level


def scatter_about(own_key, extent, spread, reach, pieces=(), dtype=jnp.bfloat16):
    result = spread * jax.random.normal(own_key, extent, jnp.float32)
    if pieces:
        result = result * level_of(own_key, extent, pieces, -0.22, 0.18)
    return jnp.clip(result, -reach, reach).astype(dtype)


def heavy_noise(stream_key, shape, scale, most, cuts, heavy, kind=jnp.bfloat16):
    drawn = scale * jax.random.normal(stream_key, shape, jnp.float32)
    if cuts:
        drawn = drawn * level_of(stream_key, shape, cuts, -0.22, 0.18)
    return jnp.clip(strengthened(drawn, jax.random.fold_in(stream_key, 3), *heavy), -most, most).astype(kind)


def setup_inputs(seed: int = 0) -> dict:
    keys = jax.random.split(jax.random.key(seed), 7)
    q_tok = draw_q_tok(jax.random.fold_in(keys[6], 71), 0)
    k_tok = draw_k_tok(jax.random.fold_in(keys[6], 71), 0)
    v_tok = scatter_about(keys[2], (SEQS, SEQ, HDH), 1.0, 6.0, ((0, 4), (1, 64)))
    d_y = heavy_noise(keys[3], (SEQS, SEQ, D), 1.0, 8.0, ((0, 4), (1, 64)), (1, 2, 64, 4.0))
    gate = jnp.clip(jnp.exp(math.log(3.0) - 2.3025851 * jax.random.uniform(keys[4], (SEQS, D), jnp.float32) ** level_of(keys[4], (SEQS, D), ((0, 4),), -0.2, 0.2)), 0.3, 3.0)
    w_out = scatter_about(keys[5], (D, HDH), HDH ** -0.5, 0.15625, ((0, 16), (1, 4)))
    return dict(q_tok=q_tok, k_tok=k_tok, v_tok=v_tok, d_y=d_y, gate=gate, w_out=w_out)


def head_columns(array, head_index):
    return array[:, head_index * HDIM:(head_index + 1) * HDIM]


def window_grads(q_seq, k_seq, v_seq, g_seq):
    softmax_scale = HDIM ** -0.5
    q_blocks = q_seq.reshape(N_BLK, BLOCK, HDIM)
    k_blocks = k_seq.reshape(N_BLK, BLOCK, HDIM)
    v_blocks = v_seq.reshape(N_BLK, BLOCK, HDIM)
    g_blocks = g_seq.reshape(N_BLK, BLOCK, HDIM)
    k_before = jnp.roll(k_blocks, 1, axis=0)
    v_before = jnp.roll(v_blocks, 1, axis=0)

    def per_block(items):
        q_rows, k_own, k_prior, v_own, v_prior, g_rows = items
        key_cat = jnp.concatenate([k_prior, k_own], axis=0)
        value_cat = jnp.concatenate([v_prior, v_own], axis=0)
        scores = jnp.dot(q_rows, key_cat.T, preferred_element_type=jnp.float32) * softmax_scale
        expo = jnp.exp(scores - jnp.max(scores, axis=1, keepdims=True))
        probs = expo / jnp.sum(expo, axis=1, keepdims=True)
        probs_half = probs.astype(jnp.bfloat16)
        attended = jnp.dot(probs_half, value_cat, preferred_element_type=jnp.float32).astype(jnp.bfloat16)
        attended_wide = lax.optimization_barrier(attended).astype(jnp.float32)
        delta = jnp.sum(g_rows.astype(jnp.float32) * attended_wide, axis=1, keepdims=True)
        prob_grad = jnp.dot(g_rows, value_cat.T, preferred_element_type=jnp.float32)
        score_grad = (probs * (prob_grad - delta)).astype(jnp.bfloat16)
        grad_q = (jnp.dot(score_grad, key_cat, preferred_element_type=jnp.float32) * softmax_scale).astype(jnp.bfloat16)
        key_part = jnp.dot(score_grad.T, q_rows, preferred_element_type=jnp.float32) * softmax_scale
        value_part = jnp.dot(probs_half.T, g_rows, preferred_element_type=jnp.float32)
        return grad_q, attended, key_part, value_part

    grad_q, attended, key_part, value_part = lax.map(
        per_block, (q_blocks, k_blocks, k_before, v_blocks, v_before, g_blocks))
    grad_k = key_part[:, BLOCK:] + jnp.roll(key_part[:, :BLOCK], -1, axis=0)
    grad_v = value_part[:, BLOCK:] + jnp.roll(value_part[:, :BLOCK], -1, axis=0)
    return (grad_q.reshape(SEQ, HDIM), grad_k.astype(jnp.bfloat16).reshape(SEQ, HDIM),
            grad_v.astype(jnp.bfloat16).reshape(SEQ, HDIM), attended.reshape(SEQ, HDIM))


def reference(q_tok, k_tok, v_tok, d_y, gate, w_out):
    def one_sequence(items):
        q_seq, k_seq, v_seq, dy_seq, gate_row = items
        scaled = (dy_seq.astype(jnp.float32) * gate_row[None, :]).astype(jnp.bfloat16)
        attn_grad = jnp.dot(scaled, w_out, preferred_element_type=jnp.float32).astype(jnp.bfloat16)
        results = [window_grads(head_columns(q_seq, head_index), head_columns(k_seq, head_index),
                                head_columns(v_seq, head_index), head_columns(attn_grad, head_index))
                   for head_index in range(HEADS)]
        grad_q = jnp.concatenate([item[0] for item in results], axis=1)
        grad_k = jnp.concatenate([item[1] for item in results], axis=1)
        grad_v = jnp.concatenate([item[2] for item in results], axis=1)
        attended = jnp.concatenate([item[3] for item in results], axis=1)
        weight_term = jnp.dot(scaled.T, attended, preferred_element_type=jnp.float32)
        return grad_q, grad_k, grad_v, weight_term

    grad_q, grad_k, grad_v, weight_terms = lax.map(one_sequence, (q_tok, k_tok, v_tok, d_y, gate))
    return grad_q, grad_k, grad_v, jnp.sum(weight_terms, axis=0)
```

```python
import functools
import itertools
import math

import jax
import jax.numpy as jnp
from jax import lax
from jax.experimental import pallas as pl
from jax.experimental.pallas import tpu as pltpu
from jax.sharding import PartitionSpec as P

HDIM = 128
BF16 = jnp.bfloat16
F32 = jnp.float32
VMEM_LIMIT = 48 * 1024 * 1024
ACROSS = (((1,), (1,)), ((), ()))
DOWN = (((0,), (0,)), ((), ()))
PLAIN = (((1,), (0,)), ((), ()))


def dot(a, b, dims):
    return lax.dot_general(a, b, dims, preferred_element_type=F32)


def params(**kw):
    return pltpu.CompilerParams(vmem_limit_bytes=VMEM_LIMIT, **kw)


def cost(flops, size, exps=0):
    return pl.CostEstimate(flops=flops, bytes_accessed=size, transcendentals=exps)


def shift(x, axis, distance):
    n = lax.axis_size(axis)
    return lax.ppermute(x, axis, [(i, (i + distance) % n) for i in range(n)])


def routed(x, axes, target):
    sizes = [lax.axis_size(a) for a in axes]

    def index(at):
        r = 0
        for a, n in zip(axes, sizes):
            r = r * n + at[a] % n
        return r

    pairs = []
    for t in itertools.product(*[range(n) for n in sizes]):
        at = dict(zip(axes, t))
        pairs.append((index(at), index({**at, **target(at)})))
    return lax.ppermute(x, tuple(axes), pairs)


def exchange(x, axis, split):
    return lax.all_to_all(x, axis, split_axis=split, concat_axis=split, tiled=True)


def forward_kernel(q_ref, k_ref, v_ref, kp_ref, vp_ref, p_ref, att_ref):
    rows = q_ref.shape[0] * q_ref.shape[1]
    flat = lambda r: r[...].reshape(rows, HDIM)
    q = flat(q_ref)
    factor = HDIM**-0.5 * math.log2(math.e)
    s_prior = dot(flat(kp_ref), q, ACROSS)
    s_own = dot(flat(k_ref), q, ACROSS)
    top = jnp.maximum(
        jnp.max(s_prior, axis=0, keepdims=True), jnp.max(s_own, axis=0, keepdims=True)
    )
    e_prior = jnp.exp2((s_prior - top) * factor)
    e_own = jnp.exp2((s_own - top) * factor)
    inv = 1.0 / (
        jnp.sum(e_prior, axis=0, keepdims=True) + jnp.sum(e_own, axis=0, keepdims=True)
    )
    p_prior = (e_prior * inv).astype(BF16)
    p_own = (e_own * inv).astype(BF16)
    p_ref[0, :rows, :] = p_prior
    p_ref[0, rows:, :] = p_own
    att_t = dot(flat(vp_ref), p_prior, DOWN) + dot(flat(v_ref), p_own, DOWN)
    att_ref[...] = att_t.T.astype(BF16)


def attention_forward(q, k, v, kp, vp):
    u, rows, width = q.shape
    heads = width // HDIM
    n = u * rows
    spec = pl.BlockSpec((u, rows, HDIM), lambda h: (0, 0, h))
    return pl.pallas_call(
        forward_kernel,
        grid=(heads,),
        in_specs=[spec] * 5,
        out_specs=[
            pl.BlockSpec((1, 2 * n, n), lambda h: (h, 0, 0)),
            pl.BlockSpec((n, HDIM), lambda h: (0, h)),
        ],
        out_shape=[
            jax.ShapeDtypeStruct((heads, 2 * n, n), BF16),
            jax.ShapeDtypeStruct((n, width), BF16),
        ],
        compiler_params=params(),
        cost_estimate=cost(8 * heads * n * n * HDIM, 12 * n * width + 4 * heads * n * n, 2 * heads * n * n),
        name="forward",
    )(q, k, v, kp, vp)


def backward_kernel(
    at_ref, q_ref, k_ref, v_ref, kp_ref, vp_ref, g_ref, p_ref, att_ref, own_ref, *rest
):
    halo_refs, (scr_k, scr_v) = rest[:4], rest[4:]
    u, part = q_ref.shape[0], q_ref.shape[1]
    rows = u * part
    flat = lambda r: r[...].reshape(rows, HDIM)
    scale = HDIM**-0.5
    q, g = flat(q_ref), g_ref[...]
    delta = jnp.sum(
        (g.astype(F32) * att_ref[...].astype(F32)).T, axis=0, keepdims=True
    )
    p_prior, p_own = p_ref[0, :rows, :], p_ref[0, rows:, :]
    ds_prior = (
        p_prior.astype(F32) * (dot(flat(vp_ref), g, ACROSS) - delta)
    ).astype(BF16)
    scr_k[...] = (dot(ds_prior, q, PLAIN) * scale).astype(BF16)
    scr_v[...] = dot(p_prior, g, PLAIN).astype(BF16)
    here = at_ref[0]
    for d in range(u):
        block = pl.ds(pl.multiple_of(lax.rem(here + d, u) * part, part), part)
        halo_refs[d][0, :, :] = scr_k[block, :]
        halo_refs[d][1, :, :] = scr_v[block, :]
    ds_own = (p_own.astype(F32) * (dot(flat(v_ref), g, ACROSS) - delta)).astype(BF16)
    dk = (dot(ds_own, q, PLAIN) * scale).astype(BF16)
    dv = dot(p_own, g, PLAIN).astype(BF16)
    dq_t = (dot(flat(kp_ref), ds_prior, DOWN) + dot(flat(k_ref), ds_own, DOWN)) * scale
    dq = dq_t.T.astype(BF16)
    for s in range(u):
        block = slice(s * part, (s + 1) * part)
        own_ref[s, 0, :, :] = dq[block, :]
        own_ref[s, 1, :, :] = dk[block, :]
        own_ref[s, 2, :, :] = dv[block, :]


def attention_backward(at, q, k, v, kp, vp, g, p, att):
    u, part, width = q.shape
    heads = width // HDIM
    n = u * part
    spec = pl.BlockSpec((u, part, HDIM), lambda h: (0, 0, h))
    flat = pl.BlockSpec((n, HDIM), lambda h: (0, h))
    return pl.pallas_call(
        backward_kernel,
        grid=(heads,),
        in_specs=[pl.BlockSpec(memory_space=pltpu.SMEM)]
        + [spec] * 5
        + [flat, pl.BlockSpec((1, 2 * n, n), lambda h: (h, 0, 0)), flat],
        out_specs=[pl.BlockSpec((u, 3, part, HDIM), lambda h: (0, 0, 0, h))]
        + [pl.BlockSpec((2, part, HDIM), lambda h: (0, 0, h))] * u,
        out_shape=[jax.ShapeDtypeStruct((u, 3, part, width), BF16)]
        + [jax.ShapeDtypeStruct((2, part, width), BF16)] * u,
        scratch_shapes=[pltpu.VMEM((n, HDIM), BF16)] * 2,
        compiler_params=params(),
        cost_estimate=cost(16 * heads * n * n * HDIM, 24 * n * width + 4 * heads * n * n),
        name="backward",
    )(at, q, k, v, kp, vp, g, p, att)


def weight_kernel(
    at_ref, own_ref, a1, a2, b1, b2, a3, b3, gate_ref, att_ref, scaled_ref, keep_ref, send_ref
):
    here, core = at_ref[0], at_ref[1]
    part = own_ref.shape[0]
    half = part // 2
    gate = gate_ref[...]

    def put(ref, distance, second):
        block = lax.rem(here + distance, 4) * part + second * half
        rows = pl.ds(pl.multiple_of(block, half), ref.shape[0])
        scaled_ref[rows, :] = (ref[...].astype(F32) * gate).astype(BF16)

    put(own_ref, 0, 0)
    put(a1, 3, 0)
    put(a2, 3, 1)
    put(b1, 1, 1)
    put(b2, 1, 0)
    put(a3, 2, 0)
    put(b3, 2, 1)
    term = dot(scaled_ref[...], att_ref[...], DOWN).astype(BF16)
    rows = term.shape[0] // 4
    first = jnp.concatenate([term[:rows], term[2 * rows : 3 * rows]], axis=0)
    second = jnp.concatenate([term[rows : 2 * rows], term[3 * rows :]], axis=0)
    keep_ref[0] = jnp.where(core == 0, first, second)
    send_ref[0] = jnp.where(core == 0, second, first)


def weight_term(at, pieces, gate, att, steps):
    part, depth = pieces[0].shape
    n, width = att.shape
    step = depth // steps
    spec = lambda r: pl.BlockSpec((r, step), lambda z: (0, z))
    out = pl.BlockSpec((1, step // 2, width), lambda z: (z, 0, 0))
    return pl.pallas_call(
        weight_kernel,
        grid=(steps,),
        in_specs=[pl.BlockSpec(memory_space=pltpu.SMEM)]
        + [spec(x.shape[0]) for x in pieces]
        + [spec(1), pl.BlockSpec((n, width), lambda z: (0, 0))],
        out_specs=[spec(n), out, out],
        out_shape=[jax.ShapeDtypeStruct((n, depth), BF16)]
        + [jax.ShapeDtypeStruct((steps, step // 2, width), BF16)] * 2,
        compiler_params=params(),
        cost_estimate=cost(2 * n * depth * width, 4 * n * depth + 2 * depth * width),
        name="weight_term",
    )(at, *pieces, gate, att)


def project_kernel(at_ref, scaled_ref, mine_ref, other_ref, g_ref, total):
    z = pl.program_id(0)
    core = at_ref[1]
    mine, other = mine_ref[0], other_ref[0]
    first = jnp.where(core == 0, mine, other)
    second = jnp.where(core == 0, other, mine)
    r = first.shape[0] // 2
    w = jnp.concatenate([first[:r], second[:r], first[r:], second[r:]], axis=0)
    term = dot(scaled_ref[...], w, PLAIN)

    @pl.when(z == 0)
    def _():
        total[...] = term

    @pl.when(z > 0)
    def _():
        total[...] += term

    @pl.when(z == pl.num_programs(0) - 1)
    def _():
        g_ref[...] = total[...].astype(BF16)


def project(at, scaled, mine, other):
    n, depth = scaled.shape
    steps, rows, width = mine.shape
    w_spec = pl.BlockSpec((1, rows, width), lambda z: (z, 0, 0))
    return pl.pallas_call(
        project_kernel,
        grid=(steps,),
        in_specs=[
            pl.BlockSpec(memory_space=pltpu.SMEM),
            pl.BlockSpec((n, depth // steps), lambda z: (0, z)),
            w_spec,
            w_spec,
        ],
        out_specs=pl.BlockSpec((n, width), lambda z: (0, 0)),
        out_shape=jax.ShapeDtypeStruct((n, width), BF16),
        scratch_shapes=[pltpu.VMEM((n, width), F32)],
        compiler_params=params(),
        cost_estimate=cost(2 * n * depth * width, 2 * n * depth + 2 * depth * width),
        name="project",
    )(at, scaled, mine, other)


def assemble_kernel(at_ref, own_ref, h0, h1, h2, h3, q_ref, k_ref, v_ref, scr):
    here = at_ref[0]
    width = own_ref.shape[3]
    for d, ref in enumerate((h0, h1, h2, h3)):
        scr[lax.rem(here + 4 - d, 4)] = ref[...]
    for s in range(4):
        cols = slice(s * width, (s + 1) * width)
        q_ref[0, :, cols] = own_ref[s, 0]
        for at, ref in ((0, k_ref), (1, v_ref)):
            ref[0, :, cols] = (
                own_ref[s, 1 + at].astype(F32) + scr[s, at].astype(F32)
            ).astype(BF16)


def assemble(at, own, halos):
    u, _, part, width = own.shape
    vmem = pl.BlockSpec(memory_space=pltpu.VMEM)
    return pl.pallas_call(
        assemble_kernel,
        in_specs=[pl.BlockSpec(memory_space=pltpu.SMEM)] + [vmem] * 5,
        out_specs=[vmem] * 3,
        out_shape=[jax.ShapeDtypeStruct((1, part, u * width), BF16)] * 3,
        scratch_shapes=[pltpu.VMEM((u, 2, part, width), BF16)],
        compiler_params=params(),
        cost_estimate=cost(2 * u * part * width, 16 * u * part * width),
        name="assemble",
    )(at, own, *halos)


def shards(q_tok, k_tok, v_tok, d_y, gate, w_out):
    uly = lax.axis_size("uly")
    n_blk = lax.axis_size("blk")
    here = lax.axis_index("uly")
    core = lax.axis_index("dp") % 2
    lower = lax.axis_index("dp") // 2
    upper = lax.axis_index("blk") % 2
    at = jnp.stack([here, core]).astype(jnp.int32)
    part = q_tok.shape[1]
    width = w_out.shape[1]
    rows = w_out.shape[0]
    along_z = [list(range(x, n_blk, 2)) for x in range(2)]
    z_size = n_blk // 2

    def to_heads(x):
        x = x[0].reshape(part, uly, width).transpose(1, 0, 2)
        return exchange(x, "uly", 0)

    w_half = lax.dynamic_slice_in_dim(w_out, core * (rows // 2), rows // 2, axis=0)
    w_far = routed(w_half, ["blk"], lambda c: dict(blk=c["blk"] ^ 1))
    w_pair = jnp.concatenate(
        [jnp.where(upper == 0, w_half, w_far), jnp.where(upper == 0, w_far, w_half)], axis=0
    )
    w_mine = lax.all_to_all(
        jnp.broadcast_to(w_pair[None], (z_size,) + w_pair.shape),
        "blk",
        split_axis=0,
        concat_axis=0,
        tiled=True,
        axis_index_groups=along_z,
    )
    swap_core = lambda x: routed(x, ["dp"], lambda c: dict(dp=c["dp"] ^ 1))
    w_other = swap_core(w_mine)

    k = to_heads(k_tok)
    v = to_heads(v_tok)
    kp = shift(k, "blk", 1)
    vp = shift(v, "blk", 1)

    dy = d_y[0]
    dy0, dy1 = dy[: part // 2], dy[part // 2 :]
    a1 = shift(dy0, "uly", 1)
    b1 = shift(dy1, "uly", -1)
    a2 = shift(dy1, "uly", 1)
    b2 = shift(dy0, "uly", -1)
    a3 = shift(a1, "uly", 1)
    b3 = shift(b1, "uly", -1)
    q = to_heads(q_tok)

    p, att = attention_forward(q, k, v, kp, vp)
    scaled, keep, send = weight_term(at, (dy, a1, a2, b1, b2, a3, b3), gate, att, z_size)

    both = (keep.astype(F32) + swap_core(send).astype(F32)).astype(BF16)
    terms = lax.all_to_all(
        both, "blk", split_axis=0, concat_axis=0, tiled=True, axis_index_groups=along_z
    )

    g = project(at, scaled, w_mine, w_other)
    own, *halos = attention_backward(at, q, k, v, kp, vp, g, p, att)
    halos = [
        routed(h, ["uly", "blk"], lambda c, d=d: dict(uly=c["uly"] + d, blk=c["blk"] - 1))
        for d, h in enumerate(halos)
    ]
    own = exchange(own, "uly", 0)
    grad_q, grad_k, grad_v = assemble(at, own, halos)

    column = jnp.sum(terms.astype(F32), axis=0).astype(BF16).reshape(2, 2, rows // 4, width)

    def x_piece(du, dl):
        piece = lax.dynamic_index_in_dim(column, upper ^ du, 0, keepdims=False)
        return lax.dynamic_index_in_dim(piece, lower ^ dl, 0, keepdims=False)

    share = x_piece(0, 0).astype(F32)
    for du, dl in ((0, 1), (1, 0), (1, 1)):
        share = share + routed(
            x_piece(du, dl),
            ["dp", "blk"],
            lambda c, du=du, dl=dl: dict(dp=c["dp"] ^ (2 * dl), blk=c["blk"] ^ du),
        ).astype(F32)
    shares = exchange(jnp.broadcast_to(share[None], (4,) + share.shape), "dp", 0)
    grad_w = (
        shares.reshape(2, 2, rows // 4, width).transpose(1, 0, 2, 3).reshape(rows, width)
    )
    return grad_q, grad_k, grad_v, grad_w


def solution(mesh):
    tokens = P("dp", ("blk", "uly"), None)
    return jax.shard_map(
        shards,
        mesh=mesh,
        in_specs=(tokens, tokens, tokens, tokens, P("dp", None), P("blk", "uly")),
        out_specs=(tokens, tokens, tokens, P("blk", "uly")),
        check_vma=False,
    )
```

```python
import functools
import itertools
import math

import jax
import jax.numpy as jnp
from jax import lax
from jax.experimental import pallas as pl
from jax.experimental.pallas import tpu as pltpu
from jax.sharding import PartitionSpec as P

HDIM = 128
BF16 = jnp.bfloat16
F32 = jnp.float32
VMEM_LIMIT = 48 * 1024 * 1024
ACROSS = (((1,), (1,)), ((), ()))
DOWN = (((0,), (0,)), ((), ()))
PLAIN = (((1,), (0,)), ((), ()))


def dot(a, b, dims):
    return lax.dot_general(a, b, dims, preferred_element_type=F32)


def params(**kw):
    return pltpu.CompilerParams(vmem_limit_bytes=VMEM_LIMIT, **kw)


def cost(flops, size, exps=0):
    return pl.CostEstimate(flops=flops, bytes_accessed=size, transcendentals=exps)


def shift(x, axis, distance):
    n = lax.axis_size(axis)
    return lax.ppermute(x, axis, [(i, (i + distance) % n) for i in range(n)])


def routed(x, axes, target):
    sizes = [lax.axis_size(a) for a in axes]

    def index(at):
        r = 0
        for a, n in zip(axes, sizes):
            r = r * n + at[a] % n
        return r

    pairs = []
    for t in itertools.product(*[range(n) for n in sizes]):
        at = dict(zip(axes, t))
        pairs.append((index(at), index({**at, **target(at)})))
    return lax.ppermute(x, tuple(axes), pairs)


def exchange(x, axis, split):
    return lax.all_to_all(x, axis, split_axis=split, concat_axis=split, tiled=True)


def forward_kernel(q_ref, k_ref, v_ref, kp_ref, vp_ref, p_ref, att_ref):
    rows = q_ref.shape[0] * q_ref.shape[1]
    flat = lambda r: r[...].reshape(rows, HDIM)
    q = flat(q_ref)
    factor = HDIM**-0.5 * math.log2(math.e)
    s_prior = dot(flat(kp_ref), q, ACROSS)
    s_own = dot(flat(k_ref), q, ACROSS)
    top = jnp.maximum(
        jnp.max(s_prior, axis=0, keepdims=True), jnp.max(s_own, axis=0, keepdims=True)
    )
    e_prior = jnp.exp2((s_prior - top) * factor)
    e_own = jnp.exp2((s_own - top) * factor)
    inv = 1.0 / (
        jnp.sum(e_prior, axis=0, keepdims=True) + jnp.sum(e_own, axis=0, keepdims=True)
    )
    p_prior = (e_prior * inv).astype(BF16)
    p_own = (e_own * inv).astype(BF16)
    p_ref[0, :rows, :] = p_prior
    p_ref[0, rows:, :] = p_own
    att_t = dot(flat(vp_ref), p_prior, DOWN) + dot(flat(v_ref), p_own, DOWN)
    att_ref[...] = att_t.T.astype(BF16)


def attention_forward(q, k, v, kp, vp):
    u, rows, width = q.shape
    heads = width // HDIM
    n = u * rows
    spec = pl.BlockSpec((u, rows, HDIM), lambda h: (0, 0, h))
    return pl.pallas_call(
        forward_kernel,
        grid=(heads,),
        in_specs=[spec] * 5,
        out_specs=[
            pl.BlockSpec((1, 2 * n, n), lambda h: (h, 0, 0)),
            pl.BlockSpec((n, HDIM), lambda h: (0, h)),
        ],
        out_shape=[
            jax.ShapeDtypeStruct((heads, 2 * n, n), BF16),
            jax.ShapeDtypeStruct((n, width), BF16),
        ],
        compiler_params=params(),
        cost_estimate=cost(8 * heads * n * n * HDIM, 12 * n * width + 4 * heads * n * n, 2 * heads * n * n),
        name="forward",
    )(q, k, v, kp, vp)


def backward_kernel(
    at_ref, q_ref, k_ref, v_ref, kp_ref, vp_ref, g_ref, p_ref, att_ref, own_ref, *rest
):
    halo_refs, (scr_k, scr_v) = rest[:4], rest[4:]
    u, part = q_ref.shape[0], q_ref.shape[1]
    rows = u * part
    flat = lambda r: r[...].reshape(rows, HDIM)
    scale = HDIM**-0.5
    q, g = flat(q_ref), g_ref[...]
    delta = jnp.sum(
        (g.astype(F32) * att_ref[...].astype(F32)).T, axis=0, keepdims=True
    )
    p_prior, p_own = p_ref[0, :rows, :], p_ref[0, rows:, :]
    ds_prior = (
        p_prior.astype(F32) * (dot(flat(vp_ref), g, ACROSS) - delta)
    ).astype(BF16)
    scr_k[...] = (dot(ds_prior, q, PLAIN) * scale).astype(BF16)
    scr_v[...] = dot(p_prior, g, PLAIN).astype(BF16)
    here = at_ref[0]
    for d in range(u):
        block = pl.ds(pl.multiple_of(lax.rem(here + d, u) * part, part), part)
        halo_refs[d][0, :, :] = scr_k[block, :]
        halo_refs[d][1, :, :] = scr_v[block, :]
    ds_own = (p_own.astype(F32) * (dot(flat(v_ref), g, ACROSS) - delta)).astype(BF16)
    dk = (dot(ds_own, q, PLAIN) * scale).astype(BF16)
    dv = dot(p_own, g, PLAIN).astype(BF16)
    dq_t = (dot(flat(kp_ref), ds_prior, DOWN) + dot(flat(k_ref), ds_own, DOWN)) * scale
    dq = dq_t.T.astype(BF16)
    for s in range(u):
        block = slice(s * part, (s + 1) * part)
        own_ref[s, 0, :, :] = dq[block, :]
        own_ref[s, 1, :, :] = dk[block, :]
        own_ref[s, 2, :, :] = dv[block, :]


def attention_backward(at, q, k, v, kp, vp, g, p, att):
    u, part, width = q.shape
    heads = width // HDIM
    n = u * part
    spec = pl.BlockSpec((u, part, HDIM), lambda h: (0, 0, h))
    flat = pl.BlockSpec((n, HDIM), lambda h: (0, h))
    return pl.pallas_call(
        backward_kernel,
        grid=(heads,),
        in_specs=[pl.BlockSpec(memory_space=pltpu.SMEM)]
        + [spec] * 5
        + [flat, pl.BlockSpec((1, 2 * n, n), lambda h: (h, 0, 0)), flat],
        out_specs=[pl.BlockSpec((u, 3, part, HDIM), lambda h: (0, 0, 0, h))]
        + [pl.BlockSpec((2, part, HDIM), lambda h: (0, 0, h))] * u,
        out_shape=[jax.ShapeDtypeStruct((u, 3, part, width), BF16)]
        + [jax.ShapeDtypeStruct((2, part, width), BF16)] * u,
        scratch_shapes=[pltpu.VMEM((n, HDIM), BF16)] * 2,
        compiler_params=params(),
        cost_estimate=cost(16 * heads * n * n * HDIM, 24 * n * width + 4 * heads * n * n),
        name="backward",
    )(at, q, k, v, kp, vp, g, p, att)


def weight_kernel(
    at_ref, own_ref, a1, a2, b1, b2, a3, b3, gate_ref, att_ref, scaled_ref, keep_ref, send_ref
):
    here, core = at_ref[0], at_ref[1]
    part = own_ref.shape[0]
    half = part // 2
    gate = gate_ref[...]

    def put(ref, distance, second):
        block = lax.rem(here + distance, 4) * part + second * half
        rows = pl.ds(pl.multiple_of(block, half), ref.shape[0])
        scaled_ref[rows, :] = (ref[...].astype(F32) * gate).astype(BF16)

    put(own_ref, 0, 0)
    put(a1, 3, 0)
    put(a2, 3, 1)
    put(b1, 1, 1)
    put(b2, 1, 0)
    put(a3, 2, 0)
    put(b3, 2, 1)
    term = dot(scaled_ref[...], att_ref[...], DOWN).astype(BF16)
    rows = term.shape[0] // 4
    first = jnp.concatenate([term[:rows], term[2 * rows : 3 * rows]], axis=0)
    second = jnp.concatenate([term[rows : 2 * rows], term[3 * rows :]], axis=0)
    keep_ref[0] = jnp.where(core == 0, first, second)
    send_ref[0] = jnp.where(core == 0, second, first)


def weight_term(at, pieces, gate, att, steps):
    part, depth = pieces[0].shape
    n, width = att.shape
    step = depth // steps
    spec = lambda r: pl.BlockSpec((r, step), lambda z: (0, z))
    out = pl.BlockSpec((1, step // 2, width), lambda z: (z, 0, 0))
    return pl.pallas_call(
        weight_kernel,
        grid=(steps,),
        in_specs=[pl.BlockSpec(memory_space=pltpu.SMEM)]
        + [spec(x.shape[0]) for x in pieces]
        + [spec(1), pl.BlockSpec((n, width), lambda z: (0, 0))],
        out_specs=[spec(n), out, out],
        out_shape=[jax.ShapeDtypeStruct((n, depth), BF16)]
        + [jax.ShapeDtypeStruct((steps, step // 2, width), BF16)] * 2,
        compiler_params=params(),
        cost_estimate=cost(2 * n * depth * width, 4 * n * depth + 2 * depth * width),
        name="weight_term",
    )(at, *pieces, gate, att)


def project_kernel(at_ref, scaled_ref, mine_ref, other_ref, g_ref, total):
    z = pl.program_id(0)
    core = at_ref[1]
    mine, other = mine_ref[0], other_ref[0]
    first = jnp.where(core == 0, mine, other)
    second = jnp.where(core == 0, other, mine)
    r = first.shape[0] // 2
    w = jnp.concatenate([first[:r], second[:r], first[r:], second[r:]], axis=0)
    term = dot(scaled_ref[...], w, PLAIN)

    @pl.when(z == 0)
    def _():
        total[...] = term

    @pl.when(z > 0)
    def _():
        total[...] += term

    @pl.when(z == pl.num_programs(0) - 1)
    def _():
        g_ref[...] = total[...].astype(BF16)


def project(at, scaled, mine, other):
    n, depth = scaled.shape
    steps, rows, width = mine.shape
    w_spec = pl.BlockSpec((1, rows, width), lambda z: (z, 0, 0))
    return pl.pallas_call(
        project_kernel,
        grid=(steps,),
        in_specs=[
            pl.BlockSpec(memory_space=pltpu.SMEM),
            pl.BlockSpec((n, depth // steps), lambda z: (0, z)),
            w_spec,
            w_spec,
        ],
        out_specs=pl.BlockSpec((n, width), lambda z: (0, 0)),
        out_shape=jax.ShapeDtypeStruct((n, width), BF16),
        scratch_shapes=[pltpu.VMEM((n, width), F32)],
        compiler_params=params(),
        cost_estimate=cost(2 * n * depth * width, 2 * n * depth + 2 * depth * width),
        name="project",
    )(at, scaled, mine, other)


def assemble_kernel(at_ref, own_ref, h0, h1, h2, h3, q_ref, k_ref, v_ref, scr):
    here = at_ref[0]
    width = own_ref.shape[3]
    for d, ref in enumerate((h0, h1, h2, h3)):
        scr[lax.rem(here + 4 - d, 4)] = ref[...]
    for s in range(4):
        cols = slice(s * width, (s + 1) * width)
        q_ref[0, :, cols] = own_ref[s, 0]
        for at, ref in ((0, k_ref), (1, v_ref)):
            ref[0, :, cols] = (
                own_ref[s, 1 + at].astype(F32) + scr[s, at].astype(F32)
            ).astype(BF16)


def assemble(at, own, halos):
    u, _, part, width = own.shape
    vmem = pl.BlockSpec(memory_space=pltpu.VMEM)
    return pl.pallas_call(
        assemble_kernel,
        in_specs=[pl.BlockSpec(memory_space=pltpu.SMEM)] + [vmem] * 5,
        out_specs=[vmem] * 3,
        out_shape=[jax.ShapeDtypeStruct((1, part, u * width), BF16)] * 3,
        scratch_shapes=[pltpu.VMEM((u, 2, part, width), BF16)],
        compiler_params=params(),
        cost_estimate=cost(2 * u * part * width, 16 * u * part * width),
        name="assemble",
    )(at, own, *halos)


SMEM = pl.BlockSpec(memory_space=pltpu.SMEM)
VMEM = pl.BlockSpec(memory_space=pltpu.VMEM)
ANY = pl.BlockSpec(memory_space=pl.ANY)


def after_those(arrays, after):
    def kernel(*refs):
        pass

    return pl.pallas_call(
        kernel,
        in_specs=[ANY] * (len(arrays) + len(after)),
        out_specs=[ANY] * len(arrays),
        out_shape=[jax.ShapeDtypeStruct(x.shape, x.dtype) for x in arrays],
        input_output_aliases={i: i for i in range(len(arrays))},
        compiler_params=params(),
        cost_estimate=cost(0, 0),
        name="gate",
    )(*arrays, *after)


def sum_kernel(at_ref, terms_ref, *refs):
    here_ref, there_ref, scr = refs[-3:]
    total = terms_ref[0].astype(F32)
    for i in range(1, terms_ref.shape[0]):
        total = total + terms_ref[i].astype(F32)
    half = here_ref.shape[0]
    scr[0] = total[:half].astype(BF16)
    scr[1] = total[half:].astype(BF16)
    here_ref[...] = scr[at_ref[3]]
    there_ref[...] = scr[1 - at_ref[3]]


def sum_terms(at, terms, after):
    steps, rows, width = terms.shape
    out = jax.ShapeDtypeStruct((rows // 2, width), BF16)
    return pl.pallas_call(
        sum_kernel,
        in_specs=[SMEM, VMEM] + [ANY] * len(after),
        out_specs=[VMEM] * 2,
        out_shape=[out, out],
        scratch_shapes=[pltpu.VMEM((2, rows // 2, width), BF16)],
        compiler_params=params(),
        cost_estimate=cost(steps * rows * width, 2 * steps * rows * width),
        name="sum_terms",
    )(at, terms, *after)


def shards(q_tok, k_tok, v_tok, d_y, gate, w_out):
    uly = lax.axis_size("uly")
    n_blk = lax.axis_size("blk")
    here = lax.axis_index("uly")
    core = lax.axis_index("dp") % 2
    lower = lax.axis_index("dp") // 2
    upper = lax.axis_index("blk") % 2
    at = jnp.stack([here, core, lower, upper]).astype(jnp.int32)
    part = q_tok.shape[1]
    width = w_out.shape[1]
    rows = w_out.shape[0]
    along_z = [list(range(x, n_blk, 2)) for x in range(2)]
    z_size = n_blk // 2

    def to_heads(x):
        x = x[0].reshape(part, uly, width).transpose(1, 0, 2)
        return exchange(x, "uly", 0)

    w_half = lax.dynamic_slice_in_dim(w_out, core * (rows // 2), rows // 2, axis=0)
    w_far = routed(w_half, ["blk"], lambda c: dict(blk=c["blk"] ^ 1))
    w_pair = jnp.concatenate(
        [jnp.where(upper == 0, w_half, w_far), jnp.where(upper == 0, w_far, w_half)], axis=0
    )
    w_mine = lax.all_to_all(
        jnp.broadcast_to(w_pair[None], (z_size,) + w_pair.shape),
        "blk",
        split_axis=0,
        concat_axis=0,
        tiled=True,
        axis_index_groups=along_z,
    )
    swap_core = lambda x: routed(x, ["dp"], lambda c: dict(dp=c["dp"] ^ 1))
    w_other = swap_core(w_mine)

    k = to_heads(k_tok)
    v = to_heads(v_tok)
    kp = shift(k, "blk", 1)
    vp = shift(v, "blk", 1)

    dy = d_y[0]
    dy0, dy1 = dy[: part // 2], dy[part // 2 :]
    a1 = shift(dy0, "uly", 1)
    b1 = shift(dy1, "uly", -1)
    a2 = shift(dy1, "uly", 1)
    b2 = shift(dy0, "uly", -1)
    a3 = shift(a1, "uly", 1)
    b3 = shift(b1, "uly", -1)
    q = to_heads(q_tok)

    p, att = attention_forward(q, k, v, kp, vp)
    scaled, keep, send = weight_term(at, (dy, a1, a2, b1, b2, a3, b3), gate, att, z_size)

    both = (keep.astype(F32) + swap_core(send).astype(F32)).astype(BF16)
    terms = lax.all_to_all(
        both, "blk", split_axis=0, concat_axis=0, tiled=True, axis_index_groups=along_z
    )

    g = project(at, scaled, w_mine, w_other)
    own, *halos = attention_backward(at, q, k, v, kp, vp, g, p, att)
    halos = [
        routed(h, ["uly", "blk"], lambda c, d=d: dict(uly=c["uly"] + d, blk=c["blk"] - 1))
        for d, h in enumerate(halos)
    ]
    (own,) = after_those([own], halos[:2])
    own = exchange(own, "uly", 0)
    grad_q, grad_k, grad_v = assemble(at, own, halos)

    here, there = sum_terms(at, terms, halos)
    near_x = routed(here, ["dp"], lambda c: dict(dp=c["dp"] ^ 2))
    far_x = [
        routed(there, ["dp", "blk"], lambda c, i=i: dict(dp=c["dp"] ^ i, blk=c["blk"] ^ 1))
        for i in (0, 2)
    ]
    mine = (here.astype(F32) + near_x.astype(F32)) + (
        far_x[0].astype(F32) + far_x[1].astype(F32)
    )
    other = swap_core(mine)
    grad_w = jnp.concatenate(
        [jnp.where(core == 0, mine, other), jnp.where(core == 0, other, mine)], axis=0
    )
    return grad_q, grad_k, grad_v, grad_w


def solution(mesh):
    tokens = P("dp", ("blk", "uly"), None)
    return jax.shard_map(
        shards,
        mesh=mesh,
        in_specs=(tokens, tokens, tokens, tokens, P("dp", None), P("blk", "uly")),
        out_specs=(tokens, tokens, tokens, P("blk", "uly")),
        check_vma=False,
    )
```

```python
import functools
import itertools
import math

import jax
import jax.numpy as jnp
from jax import lax
from jax.experimental import pallas as pl
from jax.experimental.pallas import tpu as pltpu
from jax.sharding import PartitionSpec as P

HDIM = 128
BF16 = jnp.bfloat16
F32 = jnp.float32
VMEM_LIMIT = 48 * 1024 * 1024
CHUNKS = 4
ACROSS = (((1,), (1,)), ((), ()))
DOWN = (((0,), (0,)), ((), ()))
PLAIN = (((1,), (0,)), ((), ()))


def dot(a, b, dims):
    return lax.dot_general(a, b, dims, preferred_element_type=F32)


def params(**kw):
    return pltpu.CompilerParams(vmem_limit_bytes=VMEM_LIMIT, **kw)


def cost(flops, size, exps=0):
    return pl.CostEstimate(flops=flops, bytes_accessed=size, transcendentals=exps)


def shift(x, axis, distance):
    n = lax.axis_size(axis)
    return lax.ppermute(x, axis, [(i, (i + distance) % n) for i in range(n)])


def routed(x, axes, target):
    sizes = [lax.axis_size(a) for a in axes]

    def index(at):
        r = 0
        for a, n in zip(axes, sizes):
            r = r * n + at[a] % n
        return r

    pairs = []
    for t in itertools.product(*[range(n) for n in sizes]):
        at = dict(zip(axes, t))
        pairs.append((index(at), index({**at, **target(at)})))
    return lax.ppermute(x, tuple(axes), pairs)


def exchange(x, axis, split):
    return lax.all_to_all(x, axis, split_axis=split, concat_axis=split, tiled=True)


SMEM = pl.BlockSpec(memory_space=pltpu.SMEM)
VMEM = pl.BlockSpec(memory_space=pltpu.VMEM)
ANY = pl.BlockSpec(memory_space=pl.ANY)


def after_those(arrays, after):
    def kernel(*refs):
        pass

    return pl.pallas_call(
        kernel,
        in_specs=[ANY] * (len(arrays) + len(after)),
        out_specs=[ANY] * len(arrays),
        out_shape=[jax.ShapeDtypeStruct(x.shape, x.dtype) for x in arrays],
        input_output_aliases={i: i for i in range(len(arrays))},
        compiler_params=params(),
        cost_estimate=cost(0, 0),
        name="gate",
    )(*arrays, *after)


def sum_kernel(at_ref, terms_ref, *refs):
    here_ref, there_ref, scr = refs[-3:]
    total = terms_ref[0].astype(F32)
    for i in range(1, terms_ref.shape[0]):
        total = total + terms_ref[i].astype(F32)
    half = here_ref.shape[0]
    scr[0] = total[:half].astype(BF16)
    scr[1] = total[half:].astype(BF16)
    here_ref[...] = scr[at_ref[3]]
    there_ref[...] = scr[1 - at_ref[3]]


def sum_terms(at, terms, after):
    steps, rows, width = terms.shape
    out = jax.ShapeDtypeStruct((rows // 2, width), BF16)
    return pl.pallas_call(
        sum_kernel,
        in_specs=[SMEM, VMEM] + [ANY] * len(after),
        out_specs=[VMEM] * 2,
        out_shape=[out, out],
        scratch_shapes=[pltpu.VMEM((2, rows // 2, width), BF16)],
        compiler_params=params(),
        cost_estimate=cost(steps * rows * width, 2 * steps * rows * width),
        name="sum_terms",
    )(at, terms, *after)


def cut_kernel(at_ref, k_ref, v_ref, q_ref, *rest):
    refs, scr = rest[:4], rest[4]
    part, width = refs[0].shape[1:]
    for s in range(4):
        cols = slice(s * width, (s + 1) * width)
        for i, ref in enumerate((k_ref, v_ref, q_ref)):
            scr[s, i] = ref[0, :, cols]
    for d in range(4):
        refs[d][...] = scr[lax.rem(at_ref[0] + d, 4)]


def cut(at, k, v, q):
    _, part, whole = q.shape
    width = whole // 4
    return pl.pallas_call(
        cut_kernel,
        in_specs=[SMEM] + [VMEM] * 3,
        out_specs=[VMEM] * 4,
        out_shape=[jax.ShapeDtypeStruct((3, part, width), BF16)] * 4,
        scratch_shapes=[pltpu.VMEM((4, 3, part, width), BF16)],
        compiler_params=params(),
        cost_estimate=cost(0, 12 * part * whole),
        name="cut",
    )(at, k, v, q)


def join_kernel(*refs):
    for d in range(4):
        refs[-2 + d // 2][d % 2] = refs[d][:2]


def join(kvq, after):
    _, part, width = kvq[0].shape
    return pl.pallas_call(
        join_kernel,
        in_specs=[VMEM] * 4 + [ANY] * len(after),
        out_specs=[VMEM] * 2,
        out_shape=[jax.ShapeDtypeStruct((2, 2, part, width), BF16)] * 2,
        compiler_params=params(),
        cost_estimate=cost(0, 32 * part * width),
        name="join",
    )(*kvq, *after)


def pieces_of(refs, plane):
    return jnp.concatenate([r[plane] for r in refs], axis=0)


def pairs_of(refs, plane):
    return jnp.concatenate([r[i, plane] for r in refs for i in range(2)], axis=0)


def piece_specs(part, planes):
    return [pl.BlockSpec((planes, part, HDIM), lambda h: (0, 0, h))] * 4


def pair_specs(part):
    return [pl.BlockSpec((2, 2, part, HDIM), lambda h: (0, 0, 0, h))] * 2


def flat_spec(n):
    return pl.BlockSpec((n, HDIM), lambda h: (0, h))


def head_spec(n):
    return pl.BlockSpec((1, n, n), lambda h: (h, 0, 0))


def forward_kernel(*refs):
    kvq, prior = refs[:4], refs[4:6]
    p_prior_ref, p_own_ref, att_ref = refs[-3:]
    q = pieces_of(kvq, 2)
    factor = HDIM**-0.5 * math.log2(math.e)
    s_prior = dot(pairs_of(prior, 0), q, ACROSS)
    s_own = dot(pieces_of(kvq, 0), q, ACROSS)
    top = jnp.maximum(
        jnp.max(s_prior, axis=0, keepdims=True), jnp.max(s_own, axis=0, keepdims=True)
    )
    e_prior = jnp.exp2((s_prior - top) * factor)
    e_own = jnp.exp2((s_own - top) * factor)
    inv = 1.0 / (
        jnp.sum(e_prior, axis=0, keepdims=True) + jnp.sum(e_own, axis=0, keepdims=True)
    )
    p_prior = (e_prior * inv).astype(BF16)
    p_own = (e_own * inv).astype(BF16)
    p_prior_ref[0] = p_prior
    p_own_ref[0] = p_own
    att_t = dot(pairs_of(prior, 1), p_prior, DOWN) + dot(pieces_of(kvq, 1), p_own, DOWN)
    att_ref[...] = att_t.T.astype(BF16)


def attention_forward(kvq, prior, after):
    _, part, width = kvq[0].shape
    heads, n = width // HDIM, 4 * part
    probs = jax.ShapeDtypeStruct((heads, n, n), BF16)
    return pl.pallas_call(
        forward_kernel,
        grid=(heads,),
        in_specs=piece_specs(part, 3) + pair_specs(part) + [ANY] * len(after),
        out_specs=[head_spec(n)] * 2 + [flat_spec(n)],
        out_shape=[probs, probs, jax.ShapeDtypeStruct((n, width), BF16)],
        compiler_params=params(),
        cost_estimate=cost(
            8 * heads * n * n * HDIM, 12 * n * width + 4 * heads * n * n, 2 * heads * n * n
        ),
        name="forward",
    )(*kvq, *prior, *after)


def backward_kernel(at_ref, *refs):
    kvq, prior, (g_ref, p_prior_ref, p_own_ref, att_ref) = refs[:4], refs[4:6], refs[6:10]
    own_ref, far = refs[-5], refs[-4:]
    q, g = pieces_of(kvq, 2), g_ref[...]
    part = kvq[0].shape[1]
    scale = HDIM**-0.5
    delta = jnp.sum((g.astype(F32) * att_ref[...].astype(F32)).T, axis=0, keepdims=True)
    dq_t = 0.0
    to = [lax.rem(at_ref[0] + 4 - d, 4) for d in range(4)]
    for side, keys, values, p_ref in (
        (0, pairs_of(prior, 0), pairs_of(prior, 1), p_prior_ref),
        (1, pieces_of(kvq, 0), pieces_of(kvq, 1), p_own_ref),
    ):
        p = p_ref[0]
        ds = (p.astype(F32) * (dot(values, g, ACROSS) - delta)).astype(BF16)
        dk = (dot(ds, q, PLAIN) * scale).astype(BF16)
        dv = dot(p, g, PLAIN).astype(BF16)
        for d in range(4):
            rows = slice(d * part, (d + 1) * part)
            for i, grad in enumerate((dk, dv)):
                if side:
                    own_ref[to[d], 1 + i] = grad[rows]
                else:
                    far[d][i] = grad[rows]
        dq_t = dq_t + dot(keys, ds, DOWN)
    dq = (dq_t * scale).T.astype(BF16)
    for d in range(4):
        own_ref[to[d], 0] = dq[d * part : (d + 1) * part]


def attention_backward(at, kvq, prior, g, p_prior, p_own, att):
    _, part, width = kvq[0].shape
    heads, n = width // HDIM, 4 * part
    out = pl.pallas_call(
        backward_kernel,
        grid=(heads,),
        in_specs=[SMEM]
        + piece_specs(part, 3)
        + pair_specs(part)
        + [flat_spec(n), head_spec(n), head_spec(n), flat_spec(n)],
        out_specs=[pl.BlockSpec((4, 3, part, HDIM), lambda h: (0, 0, 0, h))]
        + piece_specs(part, 2),
        out_shape=[jax.ShapeDtypeStruct((4, 3, part, width), BF16)]
        + [jax.ShapeDtypeStruct((2, part, width), BF16)] * 4,
        compiler_params=params(),
        cost_estimate=cost(16 * heads * n * n * HDIM, 24 * n * width + 4 * heads * n * n),
        name="backward",
    )(at, *kvq, *prior, g, p_prior, p_own, att)
    return out[0], out[1:]


def gated_kernel(dy_ref, gate_ref, *out_refs):
    half = out_refs[0].shape[0]
    for i, ref in enumerate(out_refs):
        rows = dy_ref[0, i * half : (i + 1) * half, :].astype(F32)
        ref[...] = (rows * gate_ref[...]).astype(BF16)


def gated(dy, gate):
    _, part, depth = dy.shape
    return pl.pallas_call(
        gated_kernel,
        out_shape=[jax.ShapeDtypeStruct((part // 2, depth), BF16)] * 2,
        compiler_params=params(),
        cost_estimate=cost(part * depth, 4 * part * depth),
        name="gated",
    )(dy, gate)


def weight_kernel(
    at_ref, o0, o1, a1, a2, b1, b2, a3, b3, att_ref, scaled_ref, keep_ref, send_ref
):
    core = at_ref[1]
    half = o0.shape[0]
    part = 2 * half

    def put(ref, distance, second):
        start = distance * part + second * half
        scaled_ref[start : start + ref.shape[0], :] = ref[...]

    put(o0, 0, 0)
    put(o1, 0, 1)
    put(a1, 1, 0)
    put(a2, 1, 1)
    put(b1, 3, 1)
    put(b2, 3, 0)
    put(a3, 2, 0)
    put(b3, 2, 1)
    step = 2 * keep_ref.shape[1]
    for z in range(keep_ref.shape[0]):
        columns = scaled_ref[:, z * step : (z + 1) * step]
        term = dot(columns, att_ref[...], DOWN).astype(BF16)
        rows = step // 4
        first = jnp.concatenate([term[:rows], term[2 * rows : 3 * rows]], axis=0)
        second = jnp.concatenate([term[rows : 2 * rows], term[3 * rows :]], axis=0)
        keep_ref[z] = jnp.where(core == 0, first, second)
        send_ref[z] = jnp.where(core == 0, second, first)


def weight_term(at, pieces, att, steps):
    _, depth = pieces[0].shape
    n, width = att.shape
    step = depth // steps
    per = CHUNKS
    spec = lambda r: pl.BlockSpec((r, per * step), lambda z: (0, z))
    out = pl.BlockSpec((per, step // 2, width), lambda z: (z, 0, 0))
    return pl.pallas_call(
        weight_kernel,
        grid=(steps // per,),
        in_specs=[pl.BlockSpec(memory_space=pltpu.SMEM)]
        + [spec(x.shape[0]) for x in pieces]
        + [pl.BlockSpec((n, width), lambda z: (0, 0))],
        out_specs=[spec(n), out, out],
        out_shape=[jax.ShapeDtypeStruct((n, depth), BF16)]
        + [jax.ShapeDtypeStruct((steps, step // 2, width), BF16)] * 2,
        compiler_params=params(),
        cost_estimate=cost(2 * n * depth * width, 4 * n * depth + 2 * depth * width),
        name="weight_term",
    )(at, *pieces, att)


def project_kernel(at_ref, scaled_ref, mine_ref, other_ref, g_ref, total):
    z = pl.program_id(0)
    core = at_ref[1]
    step = 2 * mine_ref.shape[1]
    term = 0.0
    for i in range(mine_ref.shape[0]):
        mine, other = mine_ref[i], other_ref[i]
        first = jnp.where(core == 0, mine, other)
        second = jnp.where(core == 0, other, mine)
        r = first.shape[0] // 2
        w = jnp.concatenate([first[:r], second[:r], first[r:], second[r:]], axis=0)
        term = term + dot(scaled_ref[:, i * step : (i + 1) * step], w, PLAIN)

    @pl.when(z == 0)
    def _():
        total[...] = term

    @pl.when(z > 0)
    def _():
        total[...] += term

    @pl.when(z == pl.num_programs(0) - 1)
    def _():
        g_ref[...] = total[...].astype(BF16)


def project(at, scaled, mine, other):
    n, depth = scaled.shape
    steps, rows, width = mine.shape
    per = CHUNKS
    w_spec = pl.BlockSpec((per, rows, width), lambda z: (z, 0, 0))
    return pl.pallas_call(
        project_kernel,
        grid=(steps // per,),
        in_specs=[
            pl.BlockSpec(memory_space=pltpu.SMEM),
            pl.BlockSpec((n, per * depth // steps), lambda z: (0, z)),
            w_spec,
            w_spec,
        ],
        out_specs=pl.BlockSpec((n, width), lambda z: (0, 0)),
        out_shape=jax.ShapeDtypeStruct((n, width), BF16),
        scratch_shapes=[pltpu.VMEM((n, width), F32)],
        compiler_params=params(),
        cost_estimate=cost(2 * n * depth * width, 2 * n * depth + 2 * depth * width),
        name="project",
    )(at, scaled, mine, other)


def assemble_kernel(at_ref, own_ref, h0, h1, h2, h3, q_ref, k_ref, v_ref, scr):
    here = at_ref[0]
    width = own_ref.shape[3]
    for d, ref in enumerate((h0, h1, h2, h3)):
        scr[lax.rem(here + d, 4)] = ref[...]
    for s in range(4):
        cols = slice(s * width, (s + 1) * width)
        q_ref[0, :, cols] = own_ref[s, 0]
        for at, ref in ((0, k_ref), (1, v_ref)):
            ref[0, :, cols] = (
                own_ref[s, 1 + at].astype(F32) + scr[s, at].astype(F32)
            ).astype(BF16)


def assemble(at, own, halos):
    u, _, part, width = own.shape
    vmem = pl.BlockSpec(memory_space=pltpu.VMEM)
    return pl.pallas_call(
        assemble_kernel,
        in_specs=[pl.BlockSpec(memory_space=pltpu.SMEM)] + [vmem] * 5,
        out_specs=[vmem] * 3,
        out_shape=[jax.ShapeDtypeStruct((1, part, u * width), BF16)] * 3,
        scratch_shapes=[pltpu.VMEM((u, 2, part, width), BF16)],
        compiler_params=params(),
        cost_estimate=cost(2 * u * part * width, 16 * u * part * width),
        name="assemble",
    )(at, own, *halos)


def shards(q_tok, k_tok, v_tok, d_y, gate, w_out):
    n_blk = lax.axis_size("blk")
    core, lower = lax.axis_index("dp") % 2, lax.axis_index("dp") // 2
    upper = lax.axis_index("blk") % 2
    at = jnp.stack([lax.axis_index("uly"), core, lower, upper]).astype(jnp.int32)
    rows = w_out.shape[0]
    z_size = n_blk // 2
    along_z = [list(range(x, n_blk, 2)) for x in range(2)]
    swap_core = lambda x: routed(x, ["dp"], lambda c: dict(dp=c["dp"] ^ 1))

    kvq = cut(at, k_tok, v_tok, q_tok)
    kvq = [kvq[0]] + [shift(kvq[d], "uly", d) for d in range(1, 4)]

    w_half = lax.dynamic_slice_in_dim(w_out, core * (rows // 2), rows // 2, axis=0)
    w_far = routed(w_half, ["blk"], lambda c: dict(blk=c["blk"] ^ 1))
    w_pair = jnp.concatenate(
        [jnp.where(upper == 0, w_half, w_far), jnp.where(upper == 0, w_far, w_half)], axis=0
    )
    (w_pair,) = after_those([w_pair], [kvq[1]])
    w_mine = lax.all_to_all(
        jnp.broadcast_to(w_pair[None], (z_size,) + w_pair.shape),
        "blk",
        split_axis=0,
        concat_axis=0,
        tiled=True,
        axis_index_groups=along_z,
    )
    dy0, dy1 = gated(d_y, gate)
    a1, b1 = shift(dy0, "uly", 1), shift(dy1, "uly", -1)

    prior = [shift(x, "blk", 1) for x in join(kvq, [])]
    a2, b2 = shift(dy1, "uly", 1), shift(dy0, "uly", -1)
    a3, b3 = shift(a1, "uly", 1), shift(b1, "uly", -1)
    w_other = swap_core(w_mine)

    p_prior, p_own, att = attention_forward(kvq, prior, [])
    scaled, keep, send = weight_term(at, (dy0, dy1, a1, a2, b1, b2, a3, b3), att, z_size)

    both = (keep.astype(F32) + swap_core(send).astype(F32)).astype(BF16)
    terms = lax.all_to_all(
        both, "blk", split_axis=0, concat_axis=0, tiled=True, axis_index_groups=along_z
    )

    g = project(at, scaled, w_mine, w_other)
    own, halos = attention_backward(at, kvq, prior, g, p_prior, p_own, att)
    halos = [
        routed(h, ["uly", "blk"], lambda c, d=d: dict(uly=c["uly"] - d, blk=c["blk"] - 1))
        for d, h in enumerate(halos)
    ]
    (own,) = after_those([own], halos[:1])
    own = exchange(own, "uly", 0)
    grad_q, grad_k, grad_v = assemble(at, own, halos)

    here, there = sum_terms(at, terms, halos)
    near_x = routed(here, ["dp"], lambda c: dict(dp=c["dp"] ^ 2))
    far_x = [
        routed(there, ["dp", "blk"], lambda c, i=i: dict(dp=c["dp"] ^ i, blk=c["blk"] ^ 1))
        for i in (0, 2)
    ]
    mine = (here.astype(F32) + near_x.astype(F32)) + (
        far_x[0].astype(F32) + far_x[1].astype(F32)
    )
    other = swap_core(mine)
    grad_w = jnp.concatenate(
        [jnp.where(core == 0, mine, other), jnp.where(core == 0, other, mine)], axis=0
    )
    return grad_q, grad_k, grad_v, grad_w


def solution(mesh):
    tokens = P("dp", ("blk", "uly"), None)
    return jax.shard_map(
        shards,
        mesh=mesh,
        in_specs=(tokens, tokens, tokens, tokens, P("dp", None), P("blk", "uly")),
        out_specs=(tokens, tokens, tokens, P("blk", "uly")),
        check_vma=False,
    )
```

```python
import functools
import itertools
import math

import jax
import jax.numpy as jnp
from jax import lax
from jax.experimental import pallas as pl
from jax.experimental.pallas import tpu as pltpu
from jax.sharding import PartitionSpec as P

HDIM = 128
BF16 = jnp.bfloat16
F32 = jnp.float32
VMEM_LIMIT = 48 * 1024 * 1024
CHUNKS = 4
ACROSS = (((1,), (1,)), ((), ()))
DOWN = (((0,), (0,)), ((), ()))
PLAIN = (((1,), (0,)), ((), ()))


def dot(a, b, dims):
    return lax.dot_general(a, b, dims, preferred_element_type=F32)


def params(**kw):
    return pltpu.CompilerParams(vmem_limit_bytes=VMEM_LIMIT, **kw)


def cost(flops, size, exps=0):
    return pl.CostEstimate(flops=flops, bytes_accessed=size, transcendentals=exps)


def shift(x, axis, distance):
    n = lax.axis_size(axis)
    return lax.ppermute(x, axis, [(i, (i + distance) % n) for i in range(n)])


def routed(x, axes, target):
    sizes = [lax.axis_size(a) for a in axes]

    def index(at):
        r = 0
        for a, n in zip(axes, sizes):
            r = r * n + at[a] % n
        return r

    pairs = []
    for t in itertools.product(*[range(n) for n in sizes]):
        at = dict(zip(axes, t))
        pairs.append((index(at), index({**at, **target(at)})))
    return lax.ppermute(x, tuple(axes), pairs)


def exchange(x, axis, split):
    return lax.all_to_all(x, axis, split_axis=split, concat_axis=split, tiled=True)


SMEM = pl.BlockSpec(memory_space=pltpu.SMEM)
VMEM = pl.BlockSpec(memory_space=pltpu.VMEM)
ANY = pl.BlockSpec(memory_space=pl.ANY)


def after_those(arrays, after):
    def kernel(*refs):
        pass

    return pl.pallas_call(
        kernel,
        in_specs=[ANY] * (len(arrays) + len(after)),
        out_specs=[ANY] * len(arrays),
        out_shape=[jax.ShapeDtypeStruct(x.shape, x.dtype) for x in arrays],
        input_output_aliases={i: i for i in range(len(arrays))},
        compiler_params=params(),
        cost_estimate=cost(0, 0),
        name="gate",
    )(*arrays, *after)


def sum_kernel(at_ref, terms_ref, *refs):
    here_ref, there_ref, scr = refs[-3:]
    total = terms_ref[0].astype(F32)
    for i in range(1, terms_ref.shape[0]):
        total = total + terms_ref[i].astype(F32)
    half = here_ref.shape[0]
    scr[0] = total[:half].astype(BF16)
    scr[1] = total[half:].astype(BF16)
    here_ref[...] = scr[at_ref[3]]
    there_ref[...] = scr[1 - at_ref[3]]


def sum_terms(at, terms, after):
    steps, rows, width = terms.shape
    out = jax.ShapeDtypeStruct((rows // 2, width), BF16)
    return pl.pallas_call(
        sum_kernel,
        in_specs=[SMEM, VMEM] + [ANY] * len(after),
        out_specs=[VMEM] * 2,
        out_shape=[out, out],
        scratch_shapes=[pltpu.VMEM((2, rows // 2, width), BF16)],
        compiler_params=params(),
        cost_estimate=cost(steps * rows * width, 2 * steps * rows * width),
        name="sum_terms",
    )(at, terms, *after)


def cut_kernel(at_ref, k_ref, v_ref, q_ref, *rest):
    refs, scr = rest[:4], rest[4]
    part, width = refs[0].shape[1:]
    for s in range(4):
        cols = slice(s * width, (s + 1) * width)
        for i, ref in enumerate((k_ref, v_ref, q_ref)):
            scr[s, i] = ref[0, :, cols]
    for d in range(4):
        refs[d][...] = scr[lax.rem(at_ref[0] + d, 4)]


def cut(at, k, v, q):
    _, part, whole = q.shape
    width = whole // 4
    return pl.pallas_call(
        cut_kernel,
        in_specs=[SMEM] + [VMEM] * 3,
        out_specs=[VMEM] * 4,
        out_shape=[jax.ShapeDtypeStruct((3, part, width), BF16)] * 4,
        scratch_shapes=[pltpu.VMEM((4, 3, part, width), BF16)],
        compiler_params=params(),
        cost_estimate=cost(0, 12 * part * whole),
        name="cut",
    )(at, k, v, q)


def join_kernel(*refs):
    for d in range(4):
        refs[-2 + d // 2][d % 2] = refs[d][:2]


def join(kvq, after):
    _, part, width = kvq[0].shape
    return pl.pallas_call(
        join_kernel,
        in_specs=[VMEM] * 4 + [ANY] * len(after),
        out_specs=[VMEM] * 2,
        out_shape=[jax.ShapeDtypeStruct((2, 2, part, width), BF16)] * 2,
        compiler_params=params(),
        cost_estimate=cost(0, 32 * part * width),
        name="join",
    )(*kvq, *after)


def pieces_of(refs, plane):
    return jnp.concatenate([r[plane] for r in refs], axis=0)


def pairs_of(refs, plane):
    return jnp.concatenate([r[i, plane] for r in refs for i in range(2)], axis=0)


def piece_specs(part, planes):
    return [pl.BlockSpec((planes, part, HDIM), lambda h: (0, 0, h))] * 4


def pair_specs(part):
    return [pl.BlockSpec((2, 2, part, HDIM), lambda h: (0, 0, 0, h))] * 2


def flat_spec(n):
    return pl.BlockSpec((n, HDIM), lambda h: (0, h))


def head_spec(n):
    return pl.BlockSpec((1, n, n), lambda h: (h, 0, 0))


def forward_kernel(*refs):
    kvq, prior = refs[:4], refs[4:6]
    p_prior_ref, p_own_ref, att_ref = refs[-3:]
    q = pieces_of(kvq, 2)
    factor = HDIM**-0.5 * math.log2(math.e)
    s_prior = dot(pairs_of(prior, 0), q, ACROSS)
    s_own = dot(pieces_of(kvq, 0), q, ACROSS)
    top = jnp.maximum(
        jnp.max(s_prior, axis=0, keepdims=True), jnp.max(s_own, axis=0, keepdims=True)
    )
    e_prior = jnp.exp2((s_prior - top) * factor)
    e_own = jnp.exp2((s_own - top) * factor)
    inv = 1.0 / (
        jnp.sum(e_prior, axis=0, keepdims=True) + jnp.sum(e_own, axis=0, keepdims=True)
    )
    p_prior = (e_prior * inv).astype(BF16)
    p_own = (e_own * inv).astype(BF16)
    p_prior_ref[0] = p_prior
    p_own_ref[0] = p_own
    att_t = dot(pairs_of(prior, 1), p_prior, DOWN) + dot(pieces_of(kvq, 1), p_own, DOWN)
    att_ref[...] = att_t.T.astype(BF16)


def attention_forward(kvq, prior, after):
    _, part, width = kvq[0].shape
    heads, n = width // HDIM, 4 * part
    probs = jax.ShapeDtypeStruct((heads, n, n), BF16)
    return pl.pallas_call(
        forward_kernel,
        grid=(heads,),
        in_specs=piece_specs(part, 3) + pair_specs(part) + [ANY] * len(after),
        out_specs=[head_spec(n)] * 2 + [flat_spec(n)],
        out_shape=[probs, probs, jax.ShapeDtypeStruct((n, width), BF16)],
        compiler_params=params(),
        cost_estimate=cost(
            8 * heads * n * n * HDIM, 12 * n * width + 4 * heads * n * n, 2 * heads * n * n
        ),
        name="forward",
    )(*kvq, *prior, *after)


def backward_kernel(at_ref, *refs):
    kvq, prior, (g_ref, p_prior_ref, p_own_ref, att_ref) = refs[:4], refs[4:6], refs[6:10]
    own_ref, far = refs[-5], refs[-4:]
    q, g = pieces_of(kvq, 2), g_ref[...]
    part = kvq[0].shape[1]
    scale = HDIM**-0.5
    delta = jnp.sum((g.astype(F32) * att_ref[...].astype(F32)).T, axis=0, keepdims=True)
    dq_t = 0.0
    to = [lax.rem(at_ref[0] + 4 - d, 4) for d in range(4)]
    for side, keys, values, p_ref in (
        (0, pairs_of(prior, 0), pairs_of(prior, 1), p_prior_ref),
        (1, pieces_of(kvq, 0), pieces_of(kvq, 1), p_own_ref),
    ):
        p = p_ref[0]
        ds = (p.astype(F32) * (dot(values, g, ACROSS) - delta)).astype(BF16)
        dk = (dot(ds, q, PLAIN) * scale).astype(BF16)
        dv = dot(p, g, PLAIN).astype(BF16)
        for d in range(4):
            rows = slice(d * part, (d + 1) * part)
            for i, grad in enumerate((dk, dv)):
                if side:
                    own_ref[to[d], 1 + i] = grad[rows]
                else:
                    far[d][i] = grad[rows]
        dq_t = dq_t + dot(keys, ds, DOWN)
    dq = (dq_t * scale).T.astype(BF16)
    for d in range(4):
        own_ref[to[d], 0] = dq[d * part : (d + 1) * part]


def attention_backward(at, kvq, prior, g, p_prior, p_own, att):
    _, part, width = kvq[0].shape
    heads, n = width // HDIM, 4 * part
    out = pl.pallas_call(
        backward_kernel,
        grid=(heads,),
        in_specs=[SMEM]
        + piece_specs(part, 3)
        + pair_specs(part)
        + [flat_spec(n), head_spec(n), head_spec(n), flat_spec(n)],
        out_specs=[pl.BlockSpec((4, 3, part, HDIM), lambda h: (0, 0, 0, h))]
        + piece_specs(part, 2),
        out_shape=[jax.ShapeDtypeStruct((4, 3, part, width), BF16)]
        + [jax.ShapeDtypeStruct((2, part, width), BF16)] * 4,
        compiler_params=params(),
        cost_estimate=cost(16 * heads * n * n * HDIM, 24 * n * width + 4 * heads * n * n),
        name="backward",
    )(at, *kvq, *prior, g, p_prior, p_own, att)
    return out[0], out[1:]


def gated_kernel(dy_ref, gate_ref, *out_refs):
    half = out_refs[0].shape[0]
    for i, ref in enumerate(out_refs):
        rows = dy_ref[0, i * half : (i + 1) * half, :].astype(F32)
        ref[...] = (rows * gate_ref[...]).astype(BF16)


def gated(dy, gate):
    _, part, depth = dy.shape
    return pl.pallas_call(
        gated_kernel,
        out_shape=[jax.ShapeDtypeStruct((part // 2, depth), BF16)] * 2,
        compiler_params=params(),
        cost_estimate=cost(part * depth, 4 * part * depth),
        name="gated",
    )(dy, gate)


def weight_kernel(
    at_ref, o0, o1, a1, a2, b1, b2, a3, b3, att_ref, scaled_ref, keep_ref, send_ref
):
    core = at_ref[1]
    half = o0.shape[0]
    part = 2 * half

    def put(ref, distance, second):
        start = distance * part + second * half
        scaled_ref[start : start + ref.shape[0], :] = ref[...]

    put(o0, 0, 0)
    put(o1, 0, 1)
    put(a1, 1, 0)
    put(a2, 1, 1)
    put(b1, 3, 1)
    put(b2, 3, 0)
    put(a3, 2, 0)
    put(b3, 2, 1)
    step = 2 * keep_ref.shape[1]
    for z in range(keep_ref.shape[0]):
        columns = scaled_ref[:, z * step : (z + 1) * step]
        term = dot(columns, att_ref[...], DOWN).astype(BF16)
        rows = step // 4
        first = jnp.concatenate([term[:rows], term[2 * rows : 3 * rows]], axis=0)
        second = jnp.concatenate([term[rows : 2 * rows], term[3 * rows :]], axis=0)
        keep_ref[z] = jnp.where(core == 0, first, second)
        send_ref[z] = jnp.where(core == 0, second, first)


def weight_term(at, pieces, att, steps):
    _, depth = pieces[0].shape
    n, width = att.shape
    step = depth // steps
    per = CHUNKS
    spec = lambda r: pl.BlockSpec((r, per * step), lambda z: (0, z))
    out = pl.BlockSpec((per, step // 2, width), lambda z: (z, 0, 0))
    return pl.pallas_call(
        weight_kernel,
        grid=(steps // per,),
        in_specs=[pl.BlockSpec(memory_space=pltpu.SMEM)]
        + [spec(x.shape[0]) for x in pieces]
        + [pl.BlockSpec((n, width), lambda z: (0, 0))],
        out_specs=[spec(n), out, out],
        out_shape=[jax.ShapeDtypeStruct((n, depth), BF16)]
        + [jax.ShapeDtypeStruct((steps, step // 2, width), BF16)] * 2,
        compiler_params=params(),
        cost_estimate=cost(2 * n * depth * width, 4 * n * depth + 2 * depth * width),
        name="weight_term",
    )(at, *pieces, att)


def project_kernel(at_ref, scaled_ref, mine_ref, other_ref, g_ref, total):
    z = pl.program_id(0)
    core = at_ref[1]
    step = 2 * mine_ref.shape[1]
    term = 0.0
    for i in range(mine_ref.shape[0]):
        mine, other = mine_ref[i], other_ref[i]
        first = jnp.where(core == 0, mine, other)
        second = jnp.where(core == 0, other, mine)
        r = first.shape[0] // 2
        w = jnp.concatenate([first[:r], second[:r], first[r:], second[r:]], axis=0)
        term = term + dot(scaled_ref[:, i * step : (i + 1) * step], w, PLAIN)

    @pl.when(z == 0)
    def _():
        total[...] = term

    @pl.when(z > 0)
    def _():
        total[...] += term

    @pl.when(z == pl.num_programs(0) - 1)
    def _():
        g_ref[...] = total[...].astype(BF16)


def project(at, scaled, mine, other):
    n, depth = scaled.shape
    steps, rows, width = mine.shape
    per = steps
    w_spec = pl.BlockSpec((per, rows, width), lambda z: (z, 0, 0))
    return pl.pallas_call(
        project_kernel,
        grid=(steps // per,),
        in_specs=[
            pl.BlockSpec(memory_space=pltpu.SMEM),
            pl.BlockSpec((n, per * depth // steps), lambda z: (0, z)),
            w_spec,
            w_spec,
        ],
        out_specs=pl.BlockSpec((n, width), lambda z: (0, 0)),
        out_shape=jax.ShapeDtypeStruct((n, width), BF16),
        scratch_shapes=[pltpu.VMEM((n, width), F32)],
        compiler_params=params(),
        cost_estimate=cost(2 * n * depth * width, 2 * n * depth + 2 * depth * width),
        name="project",
    )(at, scaled, mine, other)


def assemble_kernel(at_ref, own_ref, h0, h1, h2, h3, q_ref, k_ref, v_ref, scr):
    here = at_ref[0]
    width = own_ref.shape[3]
    for d, ref in enumerate((h0, h1, h2, h3)):
        scr[lax.rem(here + d, 4)] = ref[...]
    for s in range(4):
        cols = slice(s * width, (s + 1) * width)
        q_ref[0, :, cols] = own_ref[s, 0]
        for at, ref in ((0, k_ref), (1, v_ref)):
            ref[0, :, cols] = (
                own_ref[s, 1 + at].astype(F32) + scr[s, at].astype(F32)
            ).astype(BF16)


def assemble(at, own, halos):
    u, _, part, width = own.shape
    vmem = pl.BlockSpec(memory_space=pltpu.VMEM)
    return pl.pallas_call(
        assemble_kernel,
        in_specs=[pl.BlockSpec(memory_space=pltpu.SMEM)] + [vmem] * 5,
        out_specs=[vmem] * 3,
        out_shape=[jax.ShapeDtypeStruct((1, part, u * width), BF16)] * 3,
        scratch_shapes=[pltpu.VMEM((u, 2, part, width), BF16)],
        compiler_params=params(),
        cost_estimate=cost(2 * u * part * width, 16 * u * part * width),
        name="assemble",
    )(at, own, *halos)


def shards(q_tok, k_tok, v_tok, d_y, gate, w_out):
    n_blk = lax.axis_size("blk")
    core, lower = lax.axis_index("dp") % 2, lax.axis_index("dp") // 2
    upper = lax.axis_index("blk") % 2
    at = jnp.stack([lax.axis_index("uly"), core, lower, upper]).astype(jnp.int32)
    rows = w_out.shape[0]
    z_size = n_blk // 2
    along_z = [list(range(x, n_blk, 2)) for x in range(2)]
    swap_core = lambda x: routed(x, ["dp"], lambda c: dict(dp=c["dp"] ^ 1))

    kvq = cut(at, k_tok, v_tok, q_tok)
    kvq = [kvq[0]] + [shift(kvq[d], "uly", d) for d in range(1, 4)]

    w_half = lax.dynamic_slice_in_dim(w_out, core * (rows // 2), rows // 2, axis=0)
    w_far = routed(w_half, ["blk"], lambda c: dict(blk=c["blk"] ^ 1))
    w_pair = jnp.concatenate(
        [jnp.where(upper == 0, w_half, w_far), jnp.where(upper == 0, w_far, w_half)], axis=0
    )
    (w_pair,) = after_those([w_pair], [kvq[1]])
    w_mine = lax.all_to_all(
        jnp.broadcast_to(w_pair[None], (z_size,) + w_pair.shape),
        "blk",
        split_axis=0,
        concat_axis=0,
        tiled=True,
        axis_index_groups=along_z,
    )
    dy0, dy1 = gated(d_y, gate)
    a1, b1 = shift(dy0, "uly", 1), shift(dy1, "uly", -1)

    prior = [shift(x, "blk", 1) for x in join(kvq, [])]
    a2, b2 = shift(dy1, "uly", 1), shift(dy0, "uly", -1)
    a3, b3 = shift(a1, "uly", 1), shift(b1, "uly", -1)
    w_other = swap_core(w_mine)

    p_prior, p_own, att = attention_forward(kvq, prior, [])
    scaled, keep, send = weight_term(at, (dy0, dy1, a1, a2, b1, b2, a3, b3), att, z_size)

    both = (keep.astype(F32) + swap_core(send).astype(F32)).astype(BF16)
    terms = lax.all_to_all(
        both, "blk", split_axis=0, concat_axis=0, tiled=True, axis_index_groups=along_z
    )

    g = project(at, scaled, w_mine, w_other)
    own, halos = attention_backward(at, kvq, prior, g, p_prior, p_own, att)
    halos = [
        routed(h, ["uly", "blk"], lambda c, d=d: dict(uly=c["uly"] - d, blk=c["blk"] - 1))
        for d, h in enumerate(halos)
    ]
    (own,) = after_those([own], halos[:1])
    own = exchange(own, "uly", 0)
    grad_q, grad_k, grad_v = assemble(at, own, halos)

    here, there = sum_terms(at, terms, halos)
    near_x = routed(here, ["dp"], lambda c: dict(dp=c["dp"] ^ 2))
    far_x = [
        routed(there, ["dp", "blk"], lambda c, i=i: dict(dp=c["dp"] ^ i, blk=c["blk"] ^ 1))
        for i in (0, 2)
    ]
    mine = (here.astype(F32) + near_x.astype(F32)) + (
        far_x[0].astype(F32) + far_x[1].astype(F32)
    )
    other = swap_core(mine)
    grad_w = jnp.concatenate(
        [jnp.where(core == 0, mine, other), jnp.where(core == 0, other, mine)], axis=0
    )
    return grad_q, grad_k, grad_v, grad_w


def solution(mesh):
    tokens = P("dp", ("blk", "uly"), None)
    return jax.shard_map(
        shards,
        mesh=mesh,
        in_specs=(tokens, tokens, tokens, tokens, P("dp", None), P("blk", "uly")),
        out_specs=(tokens, tokens, tokens, P("blk", "uly")),
        check_vma=False,
    )
```
